32 devices in a mesh: seq: 4 (over x, core), fsdp: 4 (over z), tensor: 2 (over y).
Axes of the slice: x: 2, y: 2, z: 4, core: 2. Of those that a mesh axis runs over, the one named last changes fastest.
Arguments:
- layer_input: bfloat16 [4096, 2304], P(('seq', 'fsdp')), may hold values from -6 to 6
- positions: int32 [4096], P(('seq', 'fsdp')), may hold values from 0 to 3839, as said below
- gain_attn_in: bfloat16 [2304], P(('seq', 'fsdp')), may hold values from 0.25 to 1.75
- w_query: bfloat16 [2304, 2048], P(('seq', 'fsdp'), 'tensor'), may hold values from -0.21875 to 0.21875
- w_key: bfloat16 [2304, 1024], P(('seq', 'fsdp'), 'tensor'), may hold values from -0.21875 to 0.21875
- w_value: bfloat16 [2304, 1024], P(('seq', 'fsdp'), 'tensor'), may hold values from -0.125 to 0.125
- w_out: bfloat16 [2048, 2304], P('tensor', ('seq', 'fsdp')), may hold values from -0.125 to 0.125
- gain_attn_out: bfloat16 [2304], P(('seq', 'fsdp')), may hold values from 0.25 to 1.75
- gain_ffn_in: bfloat16 [2304], P(('seq', 'fsdp')), may hold values from 0.25 to 1.75
- w_gate: bfloat16 [2304, 9216], P(None, ('fsdp', 'tensor')), may hold values from -0.125 to 0.125
- w_up: bfloat16 [2304, 9216], P(None, ('fsdp', 'tensor')), may hold values from -0.125 to 0.125
- w_down: bfloat16 [9216, 2304], P(('fsdp', 'tensor')), may hold values from -0.0625 to 0.0625
- gain_ffn_out: bfloat16 [2304], P(('seq', 'fsdp')), may hold values from 0.25 to 1.75
- cotangent: bfloat16 [4096, 2304], P(('seq', 'fsdp', 'tensor')), may hold values from -6 to 6
Outputs:
- output: bfloat16 [4096, 2304], P(('seq', 'fsdp', 'tensor'))
- grad_input: float32 [4096, 2304], P(('seq', 'fsdp', 'tensor'))
- grad_gain_attn_in: float32 [2304], P(('seq', 'fsdp'))
- grad_w_query: float32 [2304, 2048], P(('seq', 'fsdp'), 'tensor')
- grad_w_key: float32 [2304, 1024], P(('seq', 'fsdp'), 'tensor')
- grad_w_value: float32 [2304, 1024], P(('seq', 'fsdp'), 'tensor')
- grad_w_out: float32 [2048, 2304], P('tensor', ('seq', 'fsdp'))
- grad_gain_attn_out: float32 [2304], P(('seq', 'fsdp'))
- grad_gain_ffn_in: float32 [2304], P(('seq', 'fsdp'))
- grad_w_gate: float32 [2304, 9216], P(None, ('fsdp', 'tensor'))
- grad_w_up: float32 [2304, 9216], P(None, ('fsdp', 'tensor'))
- grad_w_down: float32 [9216, 2304], P(('fsdp', 'tensor'))
- grad_gain_ffn_out: float32 [2304], P(('seq', 'fsdp'))
The draws below stay inside these ranges and needn't reach their ends.
Inputs may be any that keep to these rules, and one draw needn't show every extreme that they name: `positions`: positions restart at 0 at each document's first token and rise by one per token. One document holds exactly 3840 tokens and starts within the first 256 tokens; the tokens before it and after it form further documents, each shorter than 256 tokens.
All inputs are finite; a program needn't handle non-finite values.
Results may differ from the reference program's by a relative error of at most 0.02.
Values may be sent and summed in bfloat16 or wider, within the bound.
No kernel may reach another device: no remote copies, remote signals or barrier semaphores. Data moves between devices by JAX's collectives and lax.ppermute only.
A program may use at most 320 MiB of HBM per device.

```python
import math
import jax
import jax.numpy as jnp
from jax import lax

D = 2304
HEADS = 8
KV_HEADS = 4
HEAD = 256
FF = 9216
WINDOW = 4096
BLOCK_DEV = 256
LENGTH = 4096


def draw_positions(key, part):
    key = jax.random.fold_in(key, 7)
    cut_key = jax.random.fold_in(key, 1)
    split_key = jax.random.fold_in(key, 2)
    first_cut = jax.random.randint(cut_key, (), 1, BLOCK_DEV)
    second_cut = first_cut + (LENGTH - BLOCK_DEV)
    token_index = jnp.arange(LENGTH, dtype=jnp.int32)
    coin = jax.random.randint(split_key, (LENGTH,), 0, 8)
    outside = (token_index < first_cut) | (token_index > second_cut)
    starts_here = (token_index == 0) | (token_index == first_cut) | (token_index == second_cut)
    starts_here = starts_here | outside & (coin == 0)
    marked = jnp.where(starts_here, token_index, jnp.zeros_like(token_index))
    doc_start = lax.cummax(marked, axis=0)
    return (token_index - doc_start).astype(jnp.int32)


def steps_of(key, dims, shards, low, high):
    gain, own = 1.0, jax.random.fold_in(key, 6)
    for position, shards_of in shards:
        heights = jnp.exp(jax.random.uniform(jax.random.fold_in(own, position), (shards_of,), jnp.float32, low / len(shards), high / len(shards)))
        gain = gain * jnp.repeat(heights, dims[position] // shards_of).reshape([-1 if axis == position else 1 for axis in range(len(dims))])
    return gain


def noise(own_key, dims, width, reach, split=(), kind=jnp.bfloat16):
    values = jax.random.normal(own_key, dims, jnp.float32) * width
    if len(split) > 0:
        values = steps_of(own_key, dims, split, -0.22, 0.18) * values
    return jnp.clip(values, min=-reach, max=reach).astype(kind)


def setup_inputs(seed: int = 0) -> dict:
    arg_keys = jax.random.split(jax.random.key(seed), 15)
    return {
        "layer_input": noise(arg_keys[0], (LENGTH, D), 1.0, 6.0, ((0, 16),)),
        "positions": draw_positions(jax.random.fold_in(arg_keys[14], 71), 0),
        "gain_attn_in": jnp.clip(1.0 + 0.15 * jax.random.normal(arg_keys[2], (D,), jnp.float32), 0.25, 1.75).astype(jnp.bfloat16),
        "w_query": noise(arg_keys[3], (D, HEADS * HEAD), (D // 3) ** -0.5, 0.21875, ((0, 16), (1, 2))),
        "w_key": noise(arg_keys[4], (D, KV_HEADS * HEAD), (D // 3) ** -0.5, 0.21875, ((0, 16), (1, 2))),
        "w_value": noise(arg_keys[5], (D, KV_HEADS * HEAD), D ** -0.5, 0.125, ((0, 16), (1, 2))),
        "w_out": noise(arg_keys[6], (HEADS * HEAD, D), (HEADS * HEAD) ** -0.5, 0.125, ((0, 2), (1, 16))),
        "gain_attn_out": jnp.clip(1.0 + 0.15 * jax.random.normal(arg_keys[7], (D,), jnp.float32), 0.25, 1.75).astype(jnp.bfloat16),
        "gain_ffn_in": jnp.clip(1.0 + 0.15 * jax.random.normal(arg_keys[8], (D,), jnp.float32), 0.25, 1.75).astype(jnp.bfloat16),
        "w_gate": noise(arg_keys[9], (D, FF), D ** -0.5, 0.125, ((1, 8),)),
        "w_up": noise(arg_keys[10], (D, FF), D ** -0.5, 0.125, ((1, 8),)),
        "w_down": noise(arg_keys[11], (FF, D), FF ** -0.5, 0.0625, ((0, 8),)),
        "gain_ffn_out": jnp.clip(1.0 + 0.15 * jax.random.normal(arg_keys[12], (D,), jnp.float32), 0.25, 1.75).astype(jnp.bfloat16),
        "cotangent": noise(arg_keys[13], (LENGTH, D), 1.0, 6.0, ((0, 32),)),
    }


epsilon = 1e-06
soft_cap = 50.0
rotary_base = 10000.0

@jax.custom_vjp
def low(v):
    return lax.optimization_barrier(v.astype(jnp.bfloat16)).astype(jnp.float32)

@jax.custom_vjp
def low_back(v):
    return v

def low_keep(v):
    return (low(v), None)

def low_pass(kept, grad):
    return (grad,)

def back_keep(v):
    return (v, None)

def back_low(kept, grad):
    return (low(grad),)
low.defvjp(low_keep, low_pass)
low_back.defvjp(back_keep, back_low)

def normalize(values):
    return values * lax.rsqrt(lax.optimization_barrier(jnp.mean(values * values, axis=-1, keepdims=True)) + epsilon)

def rotary_tables(positions):
    freqs = rotary_base ** (-2.0 * jnp.arange(HEAD // 2, dtype=jnp.float32) / HEAD)
    angles = positions.astype(jnp.float32)[:, None] * freqs[None, :]
    return (jnp.cos(angles), jnp.sin(angles))

def rotate(values, cosine_table, sine_table):
    half_width = values.shape[-1] // 2
    front_half = values[..., :half_width]
    back_half = values[..., half_width:]
    cosine_part = cosine_table[:, None, :]
    sine_part = sine_table[:, None, :]
    return jnp.concatenate([front_half * cosine_part - back_half * sine_part, back_half * cosine_part + front_half * sine_part], axis=-1)

def layer(inputs, positions, gain_attn_in, w_query, w_key, w_value, w_out, gain_attn_out, gain_ffn_in, w_gate, w_up, w_down, gain_ffn_out):
    length = inputs.shape[0]
    highest = lax.Precision.HIGHEST
    normed = low(normalize(inputs) * gain_attn_in)
    query_raw = low_back(jnp.dot(normed, w_query, precision=highest))
    key_raw = low_back(jnp.dot(normed, w_key, precision=highest))
    values = low(low_back(jnp.dot(normed, w_value, precision=highest))).reshape(length, KV_HEADS, HEAD)
    cosine_table, sine_table = rotary_tables(positions)
    queries = low(rotate(query_raw.reshape(length, HEADS, HEAD), cosine_table, sine_table) * HEAD ** (-0.5))
    key_rows = low(rotate(key_raw.reshape(length, KV_HEADS, HEAD), cosine_table, sine_table))
    group_size = HEADS // KV_HEADS
    rows_block = math.gcd(512, length)
    blocks = length // rows_block
    query_blocks = queries.reshape(blocks, rows_block, KV_HEADS, group_size, HEAD)
    token_index = jnp.arange(length, dtype=jnp.int32)
    starts = jnp.arange(blocks, dtype=jnp.int32) * rows_block

    def one_block(block_pair):
        query_slice, start = block_pair
        query_places = lax.dynamic_slice_in_dim(positions, start, rows_block, 0)
        query_index = start + jnp.arange(rows_block, dtype=jnp.int32)
        place_apart = query_places[:, None] - positions[None, :]
        index_apart = query_index[:, None] - token_index[None, :]
        visible = (place_apart == index_apart) & (place_apart >= 0) & (place_apart < WINDOW)
        attention_scores = low_back(jnp.einsum('qkgd,tkd->kgqt', query_slice, key_rows, precision=highest))
        capped = soft_cap * jnp.tanh(attention_scores / soft_cap)
        capped = jnp.where(visible[None, None], capped, -1e+30)
        shifted = capped - lax.optimization_barrier(jnp.max(capped, axis=-1, keepdims=True))
        weights = jnp.exp(shifted)
        attention_output = low(weights / lax.optimization_barrier(jnp.sum(weights, axis=-1, keepdims=True)))
        return jnp.einsum('kgqt,tkd->qkgd', attention_output, values, precision=highest)
    attended = lax.map(jax.checkpoint(one_block), (query_blocks, starts))
    attended = low(low_back(attended.reshape(length, HEADS * HEAD)))
    branch = low_back(jnp.dot(attended, w_out, precision=highest))
    middle = inputs + normalize(branch) * gain_attn_out
    ffn_in = low(normalize(middle) * gain_ffn_in)
    gate = low_back(jnp.dot(ffn_in, w_gate, precision=highest))
    up_proj = low_back(jnp.dot(ffn_in, w_up, precision=highest))
    hidden = low(jax.nn.gelu(gate, approximate=True) * up_proj)
    ffn_out = low_back(jnp.dot(hidden, w_down, precision=highest))
    return middle + normalize(ffn_out) * gain_ffn_out

def reference(layer_input, positions, gain_attn_in, w_query, w_key, w_value, w_out, gain_attn_out, gain_ffn_in, w_gate, w_up, w_down, gain_ffn_out, cotangent):

    def forward(inputs, gain_one, query_w, key_w, value_w, out_w, gain_two, gain_three, gate_w, up_w, down_w, gain_four):
        return layer(inputs, positions, gain_one, query_w, key_w, value_w, out_w, gain_two, gain_three, gate_w, up_w, down_w, gain_four)
    floats = (layer_input.astype(jnp.float32), gain_attn_in.astype(jnp.float32), w_query.astype(jnp.float32), w_key.astype(jnp.float32), w_value.astype(jnp.float32), w_out.astype(jnp.float32), gain_attn_out.astype(jnp.float32), gain_ffn_in.astype(jnp.float32), w_gate.astype(jnp.float32), w_up.astype(jnp.float32), w_down.astype(jnp.float32), gain_ffn_out.astype(jnp.float32))
    output, pullback = jax.vjp(forward, *floats)
    grads = pullback(cotangent.astype(jnp.float32))
    return (output.astype(jnp.bfloat16), grads[0], grads[1], grads[2], grads[3], grads[4], grads[5], grads[6], grads[7], grads[8], grads[9], grads[10], grads[11])
```

```python
import functools

import jax
import jax.numpy as jnp
from jax import lax
from jax.experimental import pallas as pl
from jax.experimental.pallas import tpu as pltpu
from jax.sharding import PartitionSpec as P

HEAD = 256
WINDOW = 4096

epsilon = 1e-06
soft_cap = 50.0
rotary_base = 10000.0
low = jnp.bfloat16
wide = jnp.float32


def dot(left, right, left_dim=1, right_dim=0):
    return lax.dot_general(
        left, right, (((left_dim,), (right_dim,)), ((), ())), preferred_element_type=wide
    )


def unit_of(values):
    scale = lax.rsqrt(jnp.mean(values * values, axis=-1, keepdims=True) + epsilon)
    return values * scale, scale


def normalize_back(values, weighted):
    unit, scale = unit_of(values)
    grad = scale * (weighted - unit * jnp.mean(weighted * unit, axis=-1, keepdims=True))
    return grad, unit


def rotary_tables(positions):
    freqs = rotary_base ** (-2.0 * jnp.arange(HEAD // 2, dtype=wide) / HEAD)
    angles = positions.astype(wide)[:, None] * freqs[None, :]
    return jnp.cos(angles), jnp.sin(angles)


def rotate(values, cosine, sine):
    half = values.shape[-1] // 2
    front, back = values[..., :half], values[..., half:]
    return jnp.concatenate([front * cosine - back * sine, back * cosine + front * sine], axis=-1)


def gated_gelu(gate, up):
    return jax.nn.gelu(gate, approximate=True) * up


def flip(x, axis, mask):
    return lax.ppermute(x, axis, [(i, i ^ mask) for i in range(lax.axis_size(axis))])


def other_core(x):
    return flip(x, "seq", 1)


def other_x(x):
    return flip(x, "seq", 2)


def other_y(x):
    return flip(x, "tensor", 1)


PAIR = [(0, 1), (1, 0), (2, 3), (3, 2)]
MIDDLE = [(1, 2), (2, 1)]
OUTWARD = [(1, 0), (2, 3)]
INWARD = [(0, 1), (3, 2)]


def slot_places():
    count, place = lax.axis_size("fsdp"), lax.axis_index("fsdp")
    if count != 4:
        return [jnp.int32(i) for i in range(count)]
    first = place < 2
    return [place, place ^ 1, jnp.where(first, 2, 1), jnp.where(first, 3, 0)]


def own_slot():
    return 0 if lax.axis_size("fsdp") == 4 else None


def gather_slots(piece):
    count = lax.axis_size("fsdp")
    if count != 4:
        whole = lax.all_gather(piece, "fsdp", axis=0, tiled=False)
        return [whole[i] for i in range(count)]
    pair = lax.ppermute(piece, "fsdp", PAIR)
    near = lax.ppermute(piece, "fsdp", MIDDLE)
    near = near + lax.ppermute(near, "fsdp", OUTWARD)
    far = lax.ppermute(pair, "fsdp", MIDDLE)
    far = far + lax.ppermute(far, "fsdp", OUTWARD)
    return [piece, pair, near, far]


def scatter_slots(pieces):
    count = lax.axis_size("fsdp")
    if count != 4:
        return lax.psum_scatter(
            jnp.stack([p.astype(low) for p in pieces]), "fsdp", scatter_dimension=0, tiled=False
        ).astype(wide)
    own, pair, near, far = pieces

    def add(a, b):
        return a.astype(wide) + b.astype(wide)

    far = add(far, lax.ppermute(far.astype(low), "fsdp", INWARD)).astype(low)
    pair = add(pair, lax.ppermute(far, "fsdp", MIDDLE))
    near = add(near, lax.ppermute(near.astype(low), "fsdp", INWARD)).astype(low)
    own = add(own, lax.ppermute(near, "fsdp", MIDDLE))
    return add(own, lax.ppermute(pair.astype(low), "fsdp", PAIR))


def ordered(pieces, place):
    return [lax.select_n(place ^ i, *pieces) for i in range(len(pieces))]


def swap_seq(blocks, place):
    got = [lax.dynamic_index_in_dim(blocks, place, 0, False)]
    for mask in range(1, blocks.shape[0]):
        got.append(flip(lax.dynamic_index_in_dim(blocks, place ^ mask, 0, False), "seq", mask))
    return ordered(got, place)


def sum_everywhere(x):
    x = x + other_core(x)
    x = x + other_x(x)
    x = x + other_y(x)
    step = 1
    while step < lax.axis_size("fsdp"):
        x = x + flip(x, "fsdp", step)
        step *= 2
    return x


def dot_nt(left, right):
    return dot(left, right, 1, 1)


def visible_of(query_doc, key_doc, query_at, key_at, same, windowed):
    seen = query_doc == key_doc
    if same:
        seen = seen & (query_at >= key_at)
    if windowed:
        seen = seen & (query_at - key_at < WINDOW)
    return seen


def tiles(blocks, block_keys, chunk, windowed):
    reach = min(blocks - 1, (WINDOW - 2 + block_keys) // block_keys)
    return [
        [
            (key_block * block_keys + start, key_block == block)
            for key_block in range(max(0, block - reach), block + 1)
            for start in range(0, block_keys, chunk)
        ]
        for block in range(blocks)
    ]


def attend_kernel(
    plan, chunk, windowed, core, query, query_doc, query_at, keyed, key_doc, key_at, out, lse
):
    rows = query.shape[0] // len(plan)
    kind = core[0]
    for block, parts in enumerate(plan):
        here = pl.ds(block * rows, rows)
        q = query[here, :]
        total = jnp.zeros((rows, 1), wide)
        summed = jnp.zeros((rows, HEAD), wide)
        for first, same in parts:
            there = pl.ds(first, chunk)
            scores = dot_nt(q, keyed[kind, there, :])
            weights = jnp.exp(soft_cap * jnp.tanh(scores * (1.0 / soft_cap)))
            seen = visible_of(
                query_doc[here, :], key_doc[:, there], query_at[here, :], key_at[:, there], same, windowed
            )
            weights = jnp.where(seen, weights, 0.0)
            total = total + jnp.sum(weights, axis=1, keepdims=True)
            summed = summed + dot(weights.astype(low), keyed[1 - kind, there, :])
        out[here, :] = summed / total
        lse[here, :] = jnp.log(total)


def attend_back_kernel(
    plan,
    chunk,
    windowed,
    core,
    query,
    query_doc,
    query_at,
    keyed,
    key_doc,
    key_at,
    incoming,
    lse,
    delta,
    grad_query,
    grad_keyed,
    key_total,
    value_total,
):
    rows = query.shape[0] // len(plan)
    kind = core[0]
    seen_by = {}
    for block, parts in enumerate(plan):
        for first, same in parts:
            seen_by.setdefault(first, []).append((block, same))
    grad_query[...] = jnp.zeros_like(grad_query)
    for first in sorted(seen_by):
        there = pl.ds(first, chunk)
        k = keyed[kind, there, :]
        v = keyed[1 - kind, there, :]
        for turn, (block, same) in enumerate(seen_by[first]):
            here = pl.ds(block * rows, rows)
            q = query[here, :]
            d = incoming[here, :]
            bent = jnp.tanh(dot_nt(k, q) * (1.0 / soft_cap))
            weights = jnp.exp(soft_cap * bent - lse[:, here])
            seen = visible_of(
                query_doc[:, here], key_doc[there, :], query_at[:, here], key_at[there, :], same, windowed
            )
            weights = jnp.where(seen, weights, 0.0)
            grads = weights * (dot_nt(v, d) - delta[:, here]) * (1.0 - bent * bent)
            grads = grads.astype(low)
            value_part = dot(weights.astype(low), d)
            key_part = dot(grads, q)
            if turn == 0:
                value_total[...] = value_part
                key_total[...] = key_part
            else:
                value_total[...] += value_part
                key_total[...] += key_part
            grad_query[here, :] += dot(grads, k, 0, 0)
        grad_keyed[kind, there, :] = key_total[...].astype(low)
        grad_keyed[1 - kind, there, :] = value_total[...].astype(low)


def in_vmem(count):
    return [pl.BlockSpec(memory_space=pltpu.SMEM)] + [pl.BlockSpec(memory_space=pltpu.VMEM)] * count


def attend(core, query, docs, ats, keyed, key_docs, key_ats, blocks):
    tokens, keys = query.shape[0], keyed.shape[1]
    chunk = min(1024, keys // blocks)
    windowed = keys > WINDOW
    plan = tiles(blocks, keys // blocks, chunk, windowed)
    count = sum(len(parts) for parts in plan) * (tokens // blocks) * chunk
    return pl.pallas_call(
        functools.partial(attend_kernel, plan, chunk, windowed),
        out_shape=(
            jax.ShapeDtypeStruct((tokens, HEAD), wide),
            jax.ShapeDtypeStruct((tokens, 1), wide),
        ),
        in_specs=in_vmem(6),
        out_specs=(pl.BlockSpec(memory_space=pltpu.VMEM),) * 2,
        compiler_params=pltpu.CompilerParams(vmem_limit_bytes=48 * 1024 * 1024),
        cost_estimate=pl.CostEstimate(
            flops=4 * count * HEAD, bytes_accessed=6 * keys * HEAD, transcendentals=2 * count
        ),
        name="attend",
    )(core, query, docs[:, None], ats[:, None], keyed, key_docs[None, :], key_ats[None, :])


def attend_back(core, query, docs, ats, keyed, key_docs, key_ats, incoming, lse, delta, blocks):
    tokens, keys = query.shape[0], keyed.shape[1]
    chunk = min(1024, keys // blocks)
    windowed = keys > WINDOW
    plan = tiles(blocks, keys // blocks, chunk, windowed)
    count = sum(len(parts) for parts in plan) * (tokens // blocks) * chunk
    return pl.pallas_call(
        functools.partial(attend_back_kernel, plan, chunk, windowed),
        out_shape=(
            jax.ShapeDtypeStruct((tokens, HEAD), wide),
            jax.ShapeDtypeStruct(keyed.shape, low),
        ),
        in_specs=in_vmem(9),
        out_specs=(pl.BlockSpec(memory_space=pltpu.VMEM),) * 2,
        scratch_shapes=[pltpu.VMEM((chunk, HEAD), wide), pltpu.VMEM((chunk, HEAD), wide)],
        compiler_params=pltpu.CompilerParams(vmem_limit_bytes=56 * 1024 * 1024),
        cost_estimate=pl.CostEstimate(
            flops=10 * count * HEAD, bytes_accessed=12 * keys * HEAD, transcendentals=2 * count
        ),
        name="attend_back",
    )(
        core,
        query,
        docs[None, :],
        ats[None, :],
        keyed,
        key_docs[:, None],
        key_ats[:, None],
        incoming,
        lse,
        delta,
    )


def per_device(
    layer_input,
    positions,
    gain_attn_in,
    w_query,
    w_key,
    w_value,
    w_out,
    gain_attn_out,
    gain_ffn_in,
    w_gate,
    w_up,
    w_down,
    gain_ffn_out,
    cotangent,
):
    rows, width = layer_input.shape
    half_rows = cotangent.shape[0]
    blocks = lax.axis_size("seq")
    line = lax.axis_size("fsdp")
    seq_place = lax.axis_index("seq")
    fsdp_place = lax.axis_index("fsdp")
    tensor_place = lax.axis_index("tensor")
    core = seq_place % 2
    side = seq_place // 2
    share = gain_attn_in.shape[0]
    heads = w_query.shape[1] // HEAD
    places = slot_places()
    scale = HEAD ** (-0.5)
    assert blocks == heads == 4 and w_key.shape[1] == 2 * HEAD

    extra = 16
    gain_row = jnp.pad(gain_attn_in[None, :], ((0, extra - 1), (0, HEAD - share)))
    query_blocks = w_query.reshape(share, blocks, HEAD).transpose(1, 0, 2)
    keyed_blocks = jnp.stack(
        [
            jnp.concatenate(
                [(w_key, w_value)[i % 2][:, (i // 2) * HEAD : (i // 2 + 1) * HEAD], gain_row],
                axis=0,
            )
            for i in range(blocks)
        ]
    )

    def assemble(pieces):
        whole = jnp.zeros((blocks, line) + pieces[0].shape[1:], pieces[0].dtype)
        for piece, at in zip(pieces, places):
            whole = lax.dynamic_update_slice(whole, piece[:, None], (0, at, 0, 0))
        return whole.reshape(blocks * line * pieces[0].shape[1], pieces[0].shape[2])

    keyed_slots = gather_slots(jnp.stack(swap_seq(keyed_blocks, seq_place)))
    keyed_w = assemble([piece[:, :share] for piece in keyed_slots])
    gain_one = assemble([piece[:, share : share + 1, :share] for piece in keyed_slots])
    gain_one = gain_one.reshape(width).astype(wide)
    query_w = assemble(gather_slots(jnp.stack(swap_seq(query_blocks, seq_place))))

    from_x = other_x(layer_input)
    from_core = other_core(layer_input)
    from_far = other_core(from_x)
    units = [
        (unit_of(piece.astype(wide))[0] * gain_one).astype(low)
        for piece in (layer_input, from_core, from_x, from_far)
    ]
    normed = jnp.zeros((blocks, rows, width), low)
    for mask, piece in enumerate(units):
        normed = lax.dynamic_update_index_in_dim(normed, piece, seq_place ^ mask, 0)
    normed = normed.reshape(blocks * rows, width)

    place_slots = jnp.stack(gather_slots(positions))
    place_all = jnp.stack(
        ordered([place_slots] + [flip(place_slots, "seq", m) for m in range(1, blocks)], seq_place)
    )
    token_rows = jnp.arange(rows, dtype=jnp.int32)
    block_starts = jnp.arange(blocks, dtype=jnp.int32)[:, None, None] * (line * rows)
    key_at = block_starts + (jnp.stack(places) * rows)[None, :, None] + token_rows
    key_doc = (key_at - place_all).reshape(-1)
    key_at = key_at.reshape(-1)
    own = own_slot()
    own_positions = (
        place_all[:, own]
        if own is not None
        else lax.dynamic_index_in_dim(place_all, fsdp_place, 1, False)
    ).reshape(-1)
    query_at = (block_starts[:, 0] + fsdp_place * rows + token_rows).reshape(-1)
    query_doc = query_at - own_positions
    cosine, sine = rotary_tables(own_positions)
    plain = core == 1

    keyed_raw = dot(normed, keyed_w)
    keyed = jnp.where(plain, keyed_raw, rotate(keyed_raw, cosine, sine)).astype(low)
    keyed_slots = gather_slots(keyed.reshape(blocks, rows, HEAD))
    other_slots = [other_core(piece) for piece in keyed_slots]
    keyed_all = jnp.stack(
        [jnp.stack(keyed_slots, axis=1), jnp.stack(other_slots, axis=1)]
    ).reshape(2, blocks * line * rows, HEAD)
    query_raw = dot(normed, query_w)
    queries = (rotate(query_raw, cosine, sine) * scale).astype(low)
    core_array = core.reshape(1).astype(jnp.int32)

    attend_out, log_total = attend(
        core_array, queries, query_doc, query_at, keyed_all, key_doc, key_at, blocks
    )

    gains = jnp.stack([gain_attn_out, gain_ffn_in, gain_ffn_out])
    gains = jnp.pad(gains, ((0, extra - 3), (0, heads * HEAD - share)))
    out_slots = gather_slots(jnp.concatenate([w_out.T, gains], axis=0))
    out_line = jnp.zeros((line, share + extra, heads * HEAD), low)
    for piece, at in zip(out_slots, places):
        out_line = lax.dynamic_update_index_in_dim(out_line, piece, at, 0)
    out_x = other_x(out_line)
    out_core = other_core(out_line)
    out_far = other_core(out_x)
    out_w = jnp.zeros((blocks, line, share, heads * HEAD), low)
    gain_all = jnp.zeros((blocks, line, 3, share), low)
    for mask, piece in enumerate((out_line, out_core, out_x, out_far)):
        out_w = lax.dynamic_update_index_in_dim(out_w, piece[:, :share], seq_place ^ mask, 0)
        gain_all = lax.dynamic_update_index_in_dim(
            gain_all, piece[:, share : share + 3, :share], seq_place ^ mask, 0
        )
    out_w = out_w.reshape(width, heads * HEAD)
    gain_all = gain_all.transpose(2, 0, 1, 3).reshape(3, width).astype(wide)
    gain_two, gain_three, gain_four = gain_all[0], gain_all[1], gain_all[2]

    attended = jnp.concatenate(
        swap_seq(attend_out.astype(low).reshape(blocks, rows, HEAD), seq_place), axis=1
    )
    away = lax.dynamic_slice_in_dim(attended, (1 - tensor_place) * half_rows, half_rows, 0)
    kept = lax.dynamic_slice_in_dim(attended, tensor_place * half_rows, half_rows, 0)
    branch_away = other_y(dot(away, out_w, 1, 1).astype(low))
    branch = dot(kept, out_w, 1, 1) + branch_away.astype(wide)

    inputs_half = lax.dynamic_slice_in_dim(
        layer_input, tensor_place * half_rows, half_rows, 0
    ).astype(wide)
    middle = inputs_half + unit_of(branch)[0] * gain_two
    ffn_in = (unit_of(middle)[0] * gain_three).astype(low)

    def gather_rows(piece):
        return [jnp.concatenate([p, other_y(p)], axis=0) for p in gather_slots(piece)]

    def scatter_rows(parts):
        sums = [None] * len(parts)
        for i in reversed(range(len(parts))):
            got = other_y(parts[i][half_rows:].astype(low))
            sums[i] = parts[i][:half_rows].astype(wide) + got.astype(wide)
        return scatter_slots(sums)

    ffn_rows = gather_rows(ffn_in)
    gates = [dot(part, w_gate) for part in ffn_rows]
    ups = [dot(part, w_up) for part in ffn_rows]
    hiddens = [gated_gelu(g, u).astype(low) for g, u in zip(gates, ups)]
    ffn_out = scatter_rows([dot(h, w_down) for h in hiddens])
    unit_out, scale_out = unit_of(ffn_out)
    output = middle + unit_out * gain_four

    incoming = cotangent.astype(wide)
    grad_ffn_out, _ = normalize_back(ffn_out, incoming * gain_four)
    gain_four_part = jnp.sum(incoming * unit_out, axis=0)
    ffn_cots = gather_rows(grad_ffn_out.astype(low))
    grad_gates, grad_ups = [], []
    for part, g, u in zip(ffn_cots, gates, ups):
        _, pullback = jax.vjp(gated_gelu, g, u)
        grad_gate, grad_up = pullback(dot(part, w_down, 1, 1))
        grad_gates.append(grad_gate.astype(low))
        grad_ups.append(grad_up.astype(low))
    grad_ffn_in = scatter_rows(
        [dot(g, w_gate, 1, 1) + dot(u, w_up, 1, 1) for g, u in zip(grad_gates, grad_ups)]
    )

    half = width // 2
    rows_all = jnp.concatenate(ffn_rows, axis=0)
    cots_all = jnp.concatenate(ffn_cots, axis=0)
    hidden_all = jnp.concatenate(hiddens, axis=0)
    grad_gate_all = jnp.concatenate(grad_gates, axis=0)
    grad_up_all = jnp.concatenate(grad_ups, axis=0)

    def summed_over_seq(part_of, axis):
        sent = other_core(part_of((1 - core) * half).astype(low))
        mine = (part_of(core * half) + sent.astype(wide)).astype(low)
        mine = (mine.astype(wide) + other_x(mine).astype(wide)).astype(low)
        theirs = other_core(mine)
        first = jnp.where(core == 0, mine, theirs)
        second = jnp.where(core == 0, theirs, mine)
        return jnp.concatenate([first, second], axis=axis).astype(wide)

    def half_of(x, start):
        return lax.dynamic_slice_in_dim(x, start, half, 1)

    grad_down_w = summed_over_seq(lambda at: dot(hidden_all, half_of(cots_all, at), 0, 0), 1)
    grad_gate_w = summed_over_seq(lambda at: dot(half_of(rows_all, at), grad_gate_all, 0, 0), 0)
    grad_up_w = summed_over_seq(lambda at: dot(half_of(rows_all, at), grad_up_all, 0, 0), 0)

    grad_mid_norm, unit_middle = normalize_back(middle, grad_ffn_in * gain_three)
    gain_three_part = jnp.sum(grad_ffn_in * unit_middle, axis=0)
    grad_middle = incoming + grad_mid_norm
    grad_branch, unit_branch = normalize_back(branch, grad_middle * gain_two)
    gain_two_part = jnp.sum(grad_middle * unit_branch, axis=0)
    grad_branch = grad_branch.astype(low)
    branch_other = other_y(grad_branch)
    first = tensor_place == 0
    branch_cot = jnp.concatenate(
        [jnp.where(first, grad_branch, branch_other), jnp.where(first, branch_other, grad_branch)],
        axis=0,
    )
    grad_attended = dot(branch_cot, out_w).astype(low)
    grad_attended = jnp.concatenate(
        swap_seq(grad_attended.reshape(rows, blocks, HEAD).transpose(1, 0, 2), seq_place), axis=0
    )
    delta = jnp.sum(attend_out * grad_attended.astype(wide), axis=1)
    grad_queries, grad_keyed = attend_back(
        core_array,
        queries,
        query_doc,
        query_at,
        keyed_all,
        key_doc,
        key_at,
        grad_attended,
        log_total.reshape(1, -1),
        delta[None, :],
        blocks,
    )

    grad_keyed = grad_keyed.reshape(2, blocks, line, rows, HEAD)
    keyed_got = other_core(grad_keyed[1])
    keyed_sum = grad_keyed[0].astype(wide) + keyed_got.astype(wide)
    keyed_own = scatter_slots([keyed_sum[:, i] for i in range(line)]).reshape(blocks * rows, HEAD)
    grad_keyed_raw = jnp.where(plain, keyed_own, rotate(keyed_own, cosine, -sine)).astype(low)
    grad_query_raw = rotate(grad_queries * scale, cosine, -sine).astype(low)

    def to_rows(grad):
        grad = grad.astype(low).reshape(blocks, line, share, HEAD)
        parts = [lax.dynamic_index_in_dim(grad, at, 1, False) for at in places]
        return [p.astype(wide) for p in swap_seq(scatter_slots(parts).astype(low), seq_place)]

    query_grads = jnp.concatenate(to_rows(dot(normed, grad_query_raw, 0, 0)), axis=1)
    keyed_grads = to_rows(dot(normed, grad_keyed_raw, 0, 0))
    key_grads = jnp.concatenate(keyed_grads[0::2], axis=1)
    value_grads = jnp.concatenate(keyed_grads[1::2], axis=1)
    gain_one_part = (
        jnp.sum(query_grads * w_query.astype(wide), axis=1)
        + jnp.sum(key_grads * w_key.astype(wide), axis=1)
        + jnp.sum(value_grads * w_value.astype(wide), axis=1)
    )
    grad_gain_one = (gain_one_part + other_y(gain_one_part)) / gain_attn_in.astype(wide)

    out_grad = dot(branch_cot, attended, 0, 0).astype(low)
    out_grad = out_grad.reshape(2, 2, line, share, heads * HEAD)
    out_got = other_core(lax.dynamic_index_in_dim(out_grad, 1 - core, 1, False))
    out_sum = (
        lax.dynamic_index_in_dim(out_grad, core, 1, False).astype(wide) + out_got.astype(wide)
    ).astype(low)
    out_got = other_x(lax.dynamic_index_in_dim(out_sum, 1 - side, 0, False))
    out_sum = (
        lax.dynamic_index_in_dim(out_sum, side, 0, False).astype(wide) + out_got.astype(wide)
    ).astype(low)
    grad_out_w = scatter_slots(
        [lax.dynamic_index_in_dim(out_sum, at, 0, False) for at in places]
    ).T

    back = (dot(grad_query_raw, query_w, 1, 1) + dot(grad_keyed_raw, keyed_w, 1, 1)).astype(low)
    back = back.reshape(2, 2, rows, width)
    back_got = other_core(lax.dynamic_index_in_dim(back, 1 - core, 1, False))
    back = (
        lax.dynamic_index_in_dim(back, core, 1, False).astype(wide) + back_got.astype(wide)
    ).astype(low)
    back_got = other_x(lax.dynamic_index_in_dim(back, 1 - side, 0, False))
    back = (
        lax.dynamic_index_in_dim(back, side, 0, False).astype(wide) + back_got.astype(wide)
    ).astype(low)
    back_got = other_y(lax.dynamic_slice_in_dim(back, (1 - tensor_place) * half_rows, half_rows, 0))
    back = lax.dynamic_slice_in_dim(back, tensor_place * half_rows, half_rows, 0).astype(
        wide
    ) + back_got.astype(wide)
    grad_input = grad_middle + normalize_back(inputs_half, back * gain_one)[0]

    gain_sums = sum_everywhere(jnp.stack([gain_two_part, gain_three_part, gain_four_part]))
    gain_sums = lax.dynamic_slice_in_dim(gain_sums, (seq_place * line + fsdp_place) * share, share, 1)

    return (
        output.astype(low),
        grad_input,
        grad_gain_one,
        query_grads,
        key_grads,
        value_grads,
        grad_out_w,
        gain_sums[0],
        gain_sums[1],
        grad_gate_w,
        grad_up_w,
        grad_down_w,
        gain_sums[2],
    )


def solution(mesh):
    by_rows = P(("seq", "fsdp"))
    placed = (
        P(("seq", "fsdp"), None),
        by_rows,
        by_rows,
        P(("seq", "fsdp"), "tensor"),
        P(("seq", "fsdp"), "tensor"),
        P(("seq", "fsdp"), "tensor"),
        P("tensor", ("seq", "fsdp")),
        by_rows,
        by_rows,
        P(None, ("fsdp", "tensor")),
        P(None, ("fsdp", "tensor")),
        P(("fsdp", "tensor"), None),
        by_rows,
        P(("seq", "fsdp", "tensor"), None),
    )
    return jax.shard_map(
        per_device,
        mesh=mesh,
        in_specs=placed,
        out_specs=(
            P(("seq", "fsdp", "tensor"), None),
            P(("seq", "fsdp", "tensor"), None),
            by_rows,
            P(("seq", "fsdp"), "tensor"),
            P(("seq", "fsdp"), "tensor"),
            P(("seq", "fsdp"), "tensor"),
            P("tensor", ("seq", "fsdp")),
            by_rows,
            by_rows,
            P(None, ("fsdp", "tensor")),
            P(None, ("fsdp", "tensor")),
            P(("fsdp", "tensor"), None),
            by_rows,
        ),
        check_vma=False,
    )
```

```python
import functools

import jax
import jax.numpy as jnp
from jax import lax
from jax.experimental import pallas as pl
from jax.experimental.pallas import tpu as pltpu
from jax.sharding import PartitionSpec as P

HEAD = 256
WINDOW = 4096

epsilon = 1e-06
soft_cap = 50.0
rotary_base = 10000.0
low = jnp.bfloat16
wide = jnp.float32


def dot(left, right, left_dim=1, right_dim=0):
    return lax.dot_general(
        left, right, (((left_dim,), (right_dim,)), ((), ())), preferred_element_type=wide
    )


def unit_of(values):
    scale = lax.rsqrt(jnp.mean(values * values, axis=-1, keepdims=True) + epsilon)
    return values * scale, scale


def normalize_back(values, weighted):
    unit, scale = unit_of(values)
    grad = scale * (weighted - unit * jnp.mean(weighted * unit, axis=-1, keepdims=True))
    return grad, unit


def rotary_tables(positions):
    freqs = rotary_base ** (-2.0 * jnp.arange(HEAD // 2, dtype=wide) / HEAD)
    angles = positions.astype(wide)[:, None] * freqs[None, :]
    return jnp.cos(angles), jnp.sin(angles)


def rotate(values, cosine, sine):
    half = values.shape[-1] // 2
    front, back = values[..., :half], values[..., half:]
    return jnp.concatenate([front * cosine - back * sine, back * cosine + front * sine], axis=-1)


def gated_gelu(gate, up):
    return jax.nn.gelu(gate, approximate=True) * up


def flip(x, axis, mask):
    return lax.ppermute(x, axis, [(i, i ^ mask) for i in range(lax.axis_size(axis))])


def other_core(x):
    return flip(x, "seq", 1)


def other_x(x):
    return flip(x, "seq", 2)


def other_y(x):
    return flip(x, "tensor", 1)


def after(x, *others):
    if not others:
        return x
    nothing = sum(other[(0,) * other.ndim].astype(wide) * 0.0 for other in others)
    return x + nothing.astype(x.dtype)


PAIR = [(0, 1), (1, 0), (2, 3), (3, 2)]
MIDDLE = [(1, 2), (2, 1)]
OUTWARD = [(1, 0), (2, 3)]
INWARD = [(0, 1), (3, 2)]
ENDS = [(0, 3), (3, 0)]
END_TO_NEAR = [(0, 2), (3, 1)]
MIDDLE_TO_FAR = [(1, 3), (2, 0)]


def slot_places():
    count, place = lax.axis_size("fsdp"), lax.axis_index("fsdp")
    if count != 4:
        return [jnp.int32(i) for i in range(count)]
    first = place < 2
    return [place, place ^ 1, jnp.where(first, 2, 1), jnp.where(first, 3, 0)]


def gather_slots(piece):
    count = lax.axis_size("fsdp")
    if count != 4:
        whole = lax.all_gather(piece, "fsdp", axis=0, tiled=False)
        return [whole[i] for i in range(count)]
    pair = lax.ppermute(piece, "fsdp", PAIR)
    near = lax.ppermute(piece, "fsdp", MIDDLE)
    far = lax.ppermute(piece, "fsdp", ENDS) + lax.ppermute(piece, "fsdp", END_TO_NEAR)
    return [piece, pair, near + lax.ppermute(near, "fsdp", OUTWARD), far]


def gather_places(piece):
    count, place = lax.axis_size("fsdp"), lax.axis_index("fsdp")
    if count != 4:
        whole = lax.all_gather(piece, "fsdp", axis=0, tiled=False)
        return [(whole[i], jnp.int32(i)) for i in range(count)]
    got = [(piece, place)]
    for by in range(1, count):
        pairs = [(i, (i + by) % count) for i in range(count)]
        got.append((lax.ppermute(piece, "fsdp", pairs), (place - by) % count))
    return got


def scatter_start(pieces):
    count = lax.axis_size("fsdp")
    pieces = [p.astype(low) for p in pieces]
    if count != 4:
        return [lax.psum_scatter(jnp.stack(pieces), "fsdp", scatter_dimension=0, tiled=False)]
    own, pair, near, far = pieces
    near_in = lax.ppermute(near, "fsdp", INWARD)
    ends = lax.ppermute(far, "fsdp", ENDS)
    middle = lax.ppermute(far, "fsdp", MIDDLE_TO_FAR)
    pair_in = lax.ppermute(pair, "fsdp", PAIR)
    near = (near.astype(wide) + near_in.astype(wide)).astype(low)
    return [own, pair_in, ends, middle, lax.ppermute(near, "fsdp", MIDDLE)]


def scatter_end(got):
    total = got[0].astype(wide)
    for part in got[1:]:
        total = total + part.astype(wide)
    return total


def ordered(pieces, place):
    return [lax.select_n(place ^ i, *pieces) for i in range(len(pieces))]


def swap_masks(blocks, place):
    got = [lax.dynamic_index_in_dim(blocks, place, 0, False)]
    for mask in range(1, blocks.shape[0]):
        got.append(flip(lax.dynamic_index_in_dim(blocks, place ^ mask, 0, False), "seq", mask))
    return got


def swap_seq(blocks, place):
    return ordered(swap_masks(blocks, place), place)


def dot_nt(left, right):
    return dot(left, right, 1, 1)


def visible_of(query_doc, key_doc, query_at, key_at, same, windowed):
    seen = query_doc == key_doc
    if same:
        seen = seen & (query_at >= key_at)
    if windowed:
        seen = seen & (query_at - key_at < WINDOW)
    return seen


def tiles(blocks, line, rows, chunk):
    reach = min(blocks - 1, (WINDOW - 2 + line * rows) // (line * rows))
    return [
        [
            (key_block, slot, key_block == block)
            for key_block in range(max(0, block - reach), block + 1)
            for slot in range(0, line, chunk)
        ]
        for block in range(blocks)
    ]


def chunk_of(keyed, kind, key_block, slot, chunk):
    return jnp.concatenate([keyed[kind, slot + i, key_block] for i in range(chunk)], axis=0)


def attend_kernel(
    plan, chunk, windowed, core, query, query_doc, query_at, keyed, key_doc, key_at, out, lse
):
    line, rows = keyed.shape[1], keyed.shape[3]
    kind = core[0]
    for block, parts in enumerate(plan):
        here = pl.ds(block * rows, rows)
        q = query[here, :]
        total = jnp.zeros((rows, 1), wide)
        summed = jnp.zeros((rows, HEAD), wide)
        for key_block, slot, same in parts:
            there = pl.ds((key_block * line + slot) * rows, chunk * rows)
            scores = dot_nt(q, chunk_of(keyed, kind, key_block, slot, chunk))
            weights = jnp.exp(soft_cap * jnp.tanh(scores * (1.0 / soft_cap)))
            seen = visible_of(
                query_doc[here, :], key_doc[:, there], query_at[here, :], key_at[:, there], same, windowed
            )
            weights = jnp.where(seen, weights, 0.0)
            total = total + jnp.sum(weights, axis=1, keepdims=True)
            summed = summed + dot(
                weights.astype(low), chunk_of(keyed, 1 - kind, key_block, slot, chunk)
            )
        out[here, :] = summed / total
        lse[here, :] = jnp.log(total)


def attend_back_kernel(
    plan,
    chunk,
    windowed,
    core,
    query,
    query_doc,
    query_at,
    keyed,
    key_doc,
    key_at,
    incoming,
    lse,
    delta,
    grad_query,
    grad_keyed,
    key_total,
    value_total,
):
    line, rows = keyed.shape[1], keyed.shape[3]
    kind = core[0]
    seen_by = {}
    for block, parts in enumerate(plan):
        for key_block, slot, same in parts:
            seen_by.setdefault((key_block, slot), []).append((block, same))
    grad_query[...] = jnp.zeros_like(grad_query)
    for key_block, slot in sorted(seen_by):
        there = pl.ds((key_block * line + slot) * rows, chunk * rows)
        k = chunk_of(keyed, kind, key_block, slot, chunk)
        v = chunk_of(keyed, 1 - kind, key_block, slot, chunk)
        for turn, (block, same) in enumerate(seen_by[key_block, slot]):
            here = pl.ds(block * rows, rows)
            q = query[here, :]
            d = incoming[here, :]
            bent = jnp.tanh(dot_nt(k, q) * (1.0 / soft_cap))
            weights = jnp.exp(soft_cap * bent - lse[:, here])
            seen = visible_of(
                query_doc[:, here], key_doc[there, :], query_at[:, here], key_at[there, :], same, windowed
            )
            weights = jnp.where(seen, weights, 0.0)
            grads = weights * (dot_nt(v, d) - delta[:, here]) * (1.0 - bent * bent)
            grads = grads.astype(low)
            value_part = dot(weights.astype(low), d)
            key_part = dot(grads, q)
            if turn == 0:
                value_total[...] = value_part
                key_total[...] = key_part
            else:
                value_total[...] += value_part
                key_total[...] += key_part
            grad_query[here, :] += dot(grads, k, 0, 0)
        for i in range(chunk):
            inside = pl.ds(i * rows, rows)
            grad_keyed[kind, slot + i, key_block] = key_total[inside, :].astype(low)
            grad_keyed[1 - kind, slot + i, key_block] = value_total[inside, :].astype(low)


def in_vmem(count):
    return [pl.BlockSpec(memory_space=pltpu.SMEM)] + [pl.BlockSpec(memory_space=pltpu.VMEM)] * count


def kernel_sizes(keyed):
    _, line, blocks, rows, _ = keyed.shape
    chunk = min(line, max(1, 1024 // rows))
    plan = tiles(blocks, line, rows, chunk)
    count = sum(len(parts) for parts in plan) * rows * rows * chunk
    return plan, chunk, line * blocks * rows > WINDOW, count


def attend(core, query, docs, ats, keyed, key_docs, key_ats):
    tokens = query.shape[0]
    plan, chunk, windowed, count = kernel_sizes(keyed)
    return pl.pallas_call(
        functools.partial(attend_kernel, plan, chunk, windowed),
        out_shape=(
            jax.ShapeDtypeStruct((tokens, HEAD), wide),
            jax.ShapeDtypeStruct((tokens, 1), wide),
        ),
        in_specs=in_vmem(6),
        out_specs=(pl.BlockSpec(memory_space=pltpu.VMEM),) * 2,
        compiler_params=pltpu.CompilerParams(vmem_limit_bytes=48 * 1024 * 1024),
        cost_estimate=pl.CostEstimate(
            flops=4 * count * HEAD, bytes_accessed=2 * keyed.size, transcendentals=2 * count
        ),
        name="attend",
    )(core, query, docs, ats, keyed, key_docs, key_ats)


def attend_back(core, query, docs, ats, keyed, key_docs, key_ats, incoming, lse, delta):
    tokens = query.shape[0]
    plan, chunk, windowed, count = kernel_sizes(keyed)
    total = pltpu.VMEM((chunk * keyed.shape[3], HEAD), wide)
    return pl.pallas_call(
        functools.partial(attend_back_kernel, plan, chunk, windowed),
        out_shape=(
            jax.ShapeDtypeStruct((tokens, HEAD), wide),
            jax.ShapeDtypeStruct(keyed.shape, low),
        ),
        in_specs=in_vmem(9),
        out_specs=(pl.BlockSpec(memory_space=pltpu.VMEM),) * 2,
        scratch_shapes=[total, total],
        compiler_params=pltpu.CompilerParams(vmem_limit_bytes=56 * 1024 * 1024),
        cost_estimate=pl.CostEstimate(
            flops=10 * count * HEAD, bytes_accessed=4 * keyed.size, transcendentals=2 * count
        ),
        name="attend_back",
    )(
        core,
        query,
        docs,
        ats,
        keyed,
        key_docs,
        key_ats,
        incoming,
        lse,
        delta,
    )


def join_kernel(core, mine, theirs, out):
    ours = pl.program_id(0) == core[0]

    @pl.when(ours)
    def _():
        out[...] = mine[...].astype(wide)

    @pl.when(jnp.logical_not(ours))
    def _():
        out[...] = theirs[...].astype(wide)


def join_halves(core, mine, theirs):
    half, width = mine.shape
    rows = next(rows for rows in (288, 144, 72, half) if half % rows == 0)
    steps = half // rows
    return pl.pallas_call(
        join_kernel,
        out_shape=jax.ShapeDtypeStruct((2 * half, width), wide),
        grid_spec=pltpu.PrefetchScalarGridSpec(
            num_scalar_prefetch=1,
            grid=(2, steps),
            in_specs=[
                pl.BlockSpec((rows, width), lambda h, i, c: (jnp.where(h == c[0], i, 0), 0)),
                pl.BlockSpec((rows, width), lambda h, i, c: (jnp.where(h == c[0], 0, i), 0)),
            ],
            out_specs=pl.BlockSpec((rows, width), lambda h, i, c: (h * steps + i, 0)),
        ),
        compiler_params=pltpu.CompilerParams(vmem_limit_bytes=32 * 1024 * 1024),
        cost_estimate=pl.CostEstimate(flops=0, bytes_accessed=14 * half * width, transcendentals=0),
        name="join_halves",
    )(core, mine, theirs)


def per_device(
    layer_input,
    positions,
    gain_attn_in,
    w_query,
    w_key,
    w_value,
    w_out,
    gain_attn_out,
    gain_ffn_in,
    w_gate,
    w_up,
    w_down,
    gain_ffn_out,
    cotangent,
):
    rows, width = layer_input.shape
    half_rows = cotangent.shape[0]
    blocks = lax.axis_size("seq")
    line = lax.axis_size("fsdp")
    seq_place = lax.axis_index("seq")
    fsdp_place = lax.axis_index("fsdp")
    tensor_place = lax.axis_index("tensor")
    core = seq_place % 2
    side = seq_place // 2
    share = gain_attn_in.shape[0]
    heads = w_query.shape[1] // HEAD
    places = slot_places()
    scale = HEAD ** (-0.5)
    assert blocks == heads == 4 and w_key.shape[1] == 2 * HEAD

    query_blocks = w_query.reshape(share, blocks, HEAD).transpose(1, 0, 2)
    keyed_blocks = jnp.stack(
        [(w_key, w_value)[i % 2][:, (i // 2) * HEAD : (i // 2 + 1) * HEAD] for i in range(blocks)]
    )

    def assemble(pieces):
        whole = jnp.zeros((blocks, line, share, HEAD), low)
        for piece, at in pieces:
            whole = lax.dynamic_update_slice(whole, piece[:, None], (0, at, 0, 0))
        return whole.reshape(width, HEAD)

    from_x = other_x(layer_input)

    small = jnp.concatenate(
        [positions.astype(wide)]
        + [g.astype(wide) for g in (gain_attn_in, gain_attn_out, gain_ffn_in, gain_ffn_out)]
    )
    small = jnp.pad(small, (0, -small.shape[0] % 1024)).reshape(-1, 128)
    small_line = jnp.zeros((line,) + small.shape, wide)
    for piece, at in gather_places(small):
        small_line = lax.dynamic_update_index_in_dim(small_line, piece, at, 0)
    small_all = jnp.stack(
        ordered([small_line] + [flip(small_line, "seq", m) for m in range(1, blocks)], seq_place)
    ).reshape(blocks, line, -1)
    gain_one, gain_two, gain_three, gain_four = [
        small_all[:, :, rows + i * share : rows + (i + 1) * share].reshape(width) for i in range(4)
    ]
    place_all = small_all[:, :, :rows].astype(jnp.int32)

    keyed_piece = after(jnp.stack(swap_seq(keyed_blocks, seq_place)), from_x, gain_one)
    from_core = other_core(layer_input)
    from_far = other_core(from_x)

    keyed_w = assemble(gather_places(keyed_piece))
    query_piece = jnp.stack(swap_seq(query_blocks, seq_place))
    query_w = lax.all_gather(after(query_piece, keyed_w), "fsdp", axis=1, tiled=False).reshape(width, HEAD)

    out_w = lax.all_gather(after(w_out.T, keyed_piece), ("seq", "fsdp"), axis=0, tiled=True)

    normed = jnp.zeros((blocks, rows, width), low)
    for mask, piece in enumerate((layer_input, from_core, from_x, from_far)):
        unit = unit_of(piece.astype(wide))[0]
        normed = lax.dynamic_update_index_in_dim(
            normed, (unit * gain_one).astype(low), seq_place ^ mask, 0
        )
    normed = normed.reshape(blocks * rows, width)
    keyed_raw = dot(normed, keyed_w)

    token_rows = jnp.arange(rows, dtype=jnp.int32)
    block_starts = jnp.arange(blocks, dtype=jnp.int32)[:, None, None] * (line * rows)
    key_at = block_starts + (jnp.stack(places) * rows)[None, :, None] + token_rows
    key_places = jnp.stack(
        [lax.dynamic_index_in_dim(place_all, at, 1, False) for at in places], axis=1
    )
    key_doc = (key_at - key_places).reshape(-1)
    key_at = key_at.reshape(-1)
    own_positions = lax.dynamic_index_in_dim(place_all, fsdp_place, 1, False).reshape(-1)
    query_at = (block_starts[:, 0] + fsdp_place * rows + token_rows).reshape(-1)
    query_doc = query_at - own_positions
    cosine, sine = rotary_tables(own_positions)
    plain = core == 1

    keyed = jnp.where(plain, keyed_raw, rotate(keyed_raw, cosine, sine)).astype(low)
    keyed_slots = gather_slots(keyed.reshape(blocks, rows, HEAD))
    other_slots = [other_core(piece) for piece in keyed_slots]
    keyed_all = jnp.stack(keyed_slots + other_slots).reshape(2, line, blocks, rows, HEAD)
    query_raw = dot(normed, query_w)
    queries = (rotate(query_raw, cosine, sine) * scale).astype(low)
    core_array = core.reshape(1).astype(jnp.int32)

    attend_out, log_total = attend(
        core_array,
        queries,
        query_doc[:, None],
        query_at[:, None],
        keyed_all,
        key_doc[None, :],
        key_at[None, :],
    )
    back_marks = (query_doc[None, :], query_at[None, :], key_doc[:, None], key_at[:, None])
    log_total = log_total.reshape(1, -1)

    attended = jnp.concatenate(
        swap_seq(attend_out.astype(low).reshape(blocks, rows, HEAD), seq_place), axis=1
    )
    away = lax.dynamic_slice_in_dim(attended, (1 - tensor_place) * half_rows, half_rows, 0)
    kept = lax.dynamic_slice_in_dim(attended, tensor_place * half_rows, half_rows, 0)
    branch_away = other_y(dot(away, out_w, 1, 1).astype(low))
    branch = dot(kept, out_w, 1, 1) + branch_away.astype(wide)

    both_w = after(jnp.concatenate([query_w, keyed_w], axis=1), attended)
    both_all = lax.all_gather(both_w, "seq", axis=0, tiled=False)

    inputs_half = lax.dynamic_slice_in_dim(
        layer_input, tensor_place * half_rows, half_rows, 0
    ).astype(wide)
    middle = inputs_half + unit_of(branch)[0] * gain_two
    ffn_in = (unit_of(middle)[0] * gain_three).astype(low)

    def through(piece, work):
        if line != 4:
            parts = [
                work(jnp.concatenate([slot, other_y(slot)], axis=0)) for slot in gather_slots(piece)
            ]
            kept = [part[0] for part in parts]
            sums = [
                p[:half_rows] + other_y(p[half_rows:].astype(low)).astype(wide) for _, p in parts
            ]
            return kept, scatter_end(scatter_start(sums))

        def joined(one, two, *others):
            return after(jnp.concatenate([one, two], axis=0), *others)

        pair = lax.ppermute(piece, "fsdp", PAIR)
        near_middle = lax.ppermute(piece, "fsdp", MIDDLE)
        own_y = other_y(piece)
        pair_y = other_y(pair)
        far_middle = lax.ppermute(pair, "fsdp", MIDDLE)
        near_end = lax.ppermute(near_middle, "fsdp", OUTWARD)
        own_kept, own_part = work(joined(piece, own_y, pair, near_middle))
        near = near_middle + near_end
        near_y = other_y(near)
        far = far_middle + lax.ppermute(far_middle, "fsdp", OUTWARD)
        pair_kept, pair_part = work(joined(pair, pair_y, near, far_middle))
        far_y = other_y(far)
        near_kept, near_part = work(joined(near, near_y, far))
        far_kept, far_part = work(joined(far, far_y, near_part))
        kept = (own_kept, pair_kept, near_kept, far_kept)

        def sent(part, *others):
            return other_y(after(part[half_rows:].astype(low), *others))

        def added(part, got, *others):
            return after(part[:half_rows] + got.astype(wide), *others).astype(low)

        near_got = sent(near_part)
        far_got = sent(far_part)
        pair_got = sent(pair_part, far_part, near_got)
        own_got = sent(own_part, far_got)
        near_sum = added(near_part, near_got)
        near_in = lax.ppermute(near_sum, "fsdp", INWARD)
        far_sum = added(far_part, far_got)
        far_ends = lax.ppermute(far_sum, "fsdp", ENDS)
        far_middle = lax.ppermute(far_sum, "fsdp", MIDDLE_TO_FAR)
        near_sum = (near_sum.astype(wide) + near_in.astype(wide)).astype(low)
        near_middle = lax.ppermute(near_sum, "fsdp", MIDDLE)
        pair_sum = added(pair_part, pair_got)
        pair_in = lax.ppermute(pair_sum, "fsdp", PAIR)
        total = own_part[:half_rows]
        for part in (own_got, near_middle, far_ends, far_middle, pair_in):
            total = total + part.astype(wide)
        return kept, total

    def forward(part):
        gate, up = dot(part, w_gate), dot(part, w_up)
        hidden = gated_gelu(gate, up).astype(low)
        return (part, gate, up, hidden), dot(hidden, w_down)

    forward_kept, ffn_out = through(ffn_in, forward)
    ffn_out = after(ffn_out, both_all)
    unit_out, _ = unit_of(ffn_out)
    output = middle + unit_out * gain_four

    incoming = cotangent.astype(wide)
    grad_ffn_out, _ = normalize_back(ffn_out, incoming * gain_four)
    gain_four_part = jnp.sum(incoming * unit_out, axis=0)
    still = list(forward_kept)

    def backward(part):
        _, gate, up, _ = still.pop(0)
        _, pullback = jax.vjp(gated_gelu, gate, up)
        grad_gate, grad_up = pullback(dot(part, w_down, 1, 1))
        grad_gate, grad_up = grad_gate.astype(low), grad_up.astype(low)
        return (part, grad_gate, grad_up), dot(grad_gate, w_gate, 1, 1) + dot(grad_up, w_up, 1, 1)

    rows_all = jnp.concatenate([k[0] for k in forward_kept], axis=0)
    hidden_all = jnp.concatenate([k[3] for k in forward_kept], axis=0)

    def rows_product(left, rights, *others):
        return dot(left, after(jnp.concatenate(rights, axis=0), *others), 0, 0).astype(low)

    def core_half(grad):
        half = grad.shape[0] // 2
        sent = lax.dynamic_slice_in_dim(grad, (1 - core) * half, half, 0)
        kept = lax.dynamic_slice_in_dim(grad, core * half, half, 0)
        return (kept.astype(wide) + other_core(sent).astype(wide)).astype(low)

    def over_x(mine):
        return lax.psum(mine, "seq", axis_index_groups=[[0, 2], [1, 3]])

    def both_halves(mine, *hold):
        mine = after(mine, *hold)
        return join_halves(core_array, mine, other_core(mine))

    backward_kept, grad_ffn_in = through(grad_ffn_out.astype(low), backward)

    grad_mid_norm, unit_middle = normalize_back(middle, grad_ffn_in * gain_three)
    gain_three_part = jnp.sum(grad_ffn_in * unit_middle, axis=0)
    grad_middle = incoming + grad_mid_norm
    grad_branch, unit_branch = normalize_back(branch, grad_middle * gain_two)
    gain_two_part = jnp.sum(grad_middle * unit_branch, axis=0)
    grad_branch = grad_branch.astype(low)
    gain_parts = jnp.stack([gain_two_part, gain_three_part, gain_four_part])
    branch_other = other_y(grad_branch)

    down_mine = core_half(rows_product(hidden_all, [k[0] for k in backward_kept], branch_other))
    gate_mine = core_half(rows_product(rows_all, [k[1] for k in backward_kept], grad_branch))
    up_mine = core_half(rows_product(rows_all, [k[2] for k in backward_kept], branch_other))
    down_sum, gate_sum, up_sum = over_x((down_mine, gate_mine, up_mine))

    always = positions[0] >= 0

    def stretch(work):
        shapes = jax.eval_shape(work)
        return lax.cond(
            always, work, lambda: jax.tree.map(lambda x: jnp.zeros(x.shape, x.dtype), shapes)
        )

    def attention_back():
        gains = gain_parts + other_y(gain_parts)
        first = tensor_place == 0
        branch_cot = jnp.concatenate(
            [
                jnp.where(first, grad_branch, branch_other),
                jnp.where(first, branch_other, grad_branch),
            ],
            axis=0,
        )
        grad_attended = dot(branch_cot, out_w).astype(low)
        grad_attended = jnp.concatenate(
            swap_seq(grad_attended.reshape(rows, blocks, HEAD).transpose(1, 0, 2), seq_place), axis=0
        )
        delta = jnp.sum(attend_out * grad_attended.astype(wide), axis=1)
        grad_queries, grad_keyed = attend_back(
            core_array,
            queries,
            *back_marks[:2],
            keyed_all,
            *back_marks[2:],
            grad_attended,
            log_total,
            delta[None, :],
        )
        keyed_got = other_core(grad_keyed[1])
        keyed_started = scatter_start(
            [grad_keyed[0, i].astype(wide) + keyed_got[i].astype(wide) for i in range(line)]
        )
        grad_query_raw = rotate(grad_queries * scale, cosine, -sine).astype(low)

        extra = 16
        gain_rows = gains.reshape(3, 2, 2, line, share).transpose(2, 3, 1, 0, 4)
        gain_rows = gain_rows.reshape(2, line, 2, 1, 3 * share).astype(low)
        gain_rows = jnp.pad(
            gain_rows, ((0, 0),) * 3 + ((0, extra - 1), (0, heads * HEAD - 3 * share))
        )
        out_grad = dot(after(branch_cot, grad_queries), attended, 0, 0).astype(low)
        out_grad = out_grad.reshape(2, 2, line, share, heads * HEAD).transpose(1, 2, 0, 3, 4)
        out_grad = jnp.concatenate([out_grad, gain_rows], axis=3)
        out_got = other_core(lax.dynamic_index_in_dim(out_grad, 1 - core, 0, False))
        out_sum = lax.dynamic_index_in_dim(out_grad, core, 0, False).astype(wide)
        out_sum = (out_sum + out_got.astype(wide)).astype(low)

        keyed_own = scatter_end(keyed_started).reshape(blocks * rows, HEAD)
        grad_keyed_raw = jnp.where(plain, keyed_own, rotate(keyed_own, cosine, -sine)).astype(low)
        return jnp.concatenate([grad_query_raw, grad_keyed_raw], axis=1), out_sum

    grad_raw, out_sum = stretch(attention_back)

    weight_grad = dot(normed, grad_raw, 0, 0).astype(low).reshape(blocks, line, share, 2 * HEAD)
    weight_started = scatter_start(
        [lax.dynamic_index_in_dim(weight_grad, at, 1, False) for at in places]
    )

    raw_mine = swap_seq(grad_raw.reshape(blocks, rows, 2 * HEAD), seq_place)
    back = sum(dot(part, both_all[i], 1, 1) for i, part in enumerate(raw_mine))
    back_got = other_y(
        lax.dynamic_slice_in_dim(back, (1 - tensor_place) * half_rows, half_rows, 0).astype(low)
    )
    back = lax.dynamic_slice_in_dim(back, tensor_place * half_rows, half_rows, 0)
    back = back + back_got.astype(wide)
    grad_input = grad_middle + normalize_back(inputs_half, back * gain_one)[0]

    out_parts = after(out_sum, weight_grad)
    out_started = scatter_start(
        [lax.dynamic_index_in_dim(out_parts, at, 0, False) for at in places]
    )
    weight_sum = scatter_end(weight_started).astype(low)
    out_sum = scatter_end(out_started)
    out_got = other_x(lax.dynamic_index_in_dim(out_sum, 1 - side, 0, False).astype(low))
    weight_grads = [part.astype(wide) for part in swap_seq(weight_sum, seq_place)]
    query_grads = jnp.concatenate([part[:, :HEAD] for part in weight_grads], axis=1)
    key_grads = jnp.concatenate([part[:, HEAD:] for part in weight_grads[0::2]], axis=1)
    value_grads = jnp.concatenate([part[:, HEAD:] for part in weight_grads[1::2]], axis=1)
    gain_one_part = (
        jnp.sum(query_grads * w_query.astype(wide), axis=1)
        + jnp.sum(key_grads * w_key.astype(wide), axis=1)
        + jnp.sum(value_grads * w_value.astype(wide), axis=1)
    )
    grad_gain_one = (gain_one_part + other_y(gain_one_part)) / gain_attn_in.astype(wide)
    out_sum = lax.dynamic_index_in_dim(out_sum, side, 0, False) + out_got.astype(wide)
    gain_sums = out_sum[share, : 3 * share].reshape(3, share)

    return (
        output.astype(low),
        grad_input,
        grad_gain_one,
        query_grads,
        key_grads,
        value_grads,
        out_sum[:share].T,
        gain_sums[0],
        gain_sums[1],
        both_halves(gate_sum, weight_started[:3][-1]),
        both_halves(up_sum, weight_started[:3][-1]),
        both_halves(down_sum, weight_started[:3][-1]),
        gain_sums[2],
    )


def solution(mesh):
    by_rows = P(("seq", "fsdp"))
    placed = (
        P(("seq", "fsdp"), None),
        by_rows,
        by_rows,
        P(("seq", "fsdp"), "tensor"),
        P(("seq", "fsdp"), "tensor"),
        P(("seq", "fsdp"), "tensor"),
        P("tensor", ("seq", "fsdp")),
        by_rows,
        by_rows,
        P(None, ("fsdp", "tensor")),
        P(None, ("fsdp", "tensor")),
        P(("fsdp", "tensor"), None),
        by_rows,
        P(("seq", "fsdp", "tensor"), None),
    )
    return jax.shard_map(
        per_device,
        mesh=mesh,
        in_specs=placed,
        out_specs=(
            P(("seq", "fsdp", "tensor"), None),
            P(("seq", "fsdp", "tensor"), None),
            by_rows,
            P(("seq", "fsdp"), "tensor"),
            P(("seq", "fsdp"), "tensor"),
            P(("seq", "fsdp"), "tensor"),
            P("tensor", ("seq", "fsdp")),
            by_rows,
            by_rows,
            P(None, ("fsdp", "tensor")),
            P(None, ("fsdp", "tensor")),
            P(("fsdp", "tensor"), None),
            by_rows,
        ),
        check_vma=False,
    )
```

```python
import functools

import jax
import jax.numpy as jnp
from jax import lax
from jax.experimental import pallas as pl
from jax.experimental.pallas import tpu as pltpu
from jax.sharding import PartitionSpec as P

HEAD = 256
WINDOW = 4096

epsilon = 1e-06
soft_cap = 50.0
rotary_base = 10000.0
low = jnp.bfloat16
wide = jnp.float32


def dot(left, right, left_dim=1, right_dim=0):
    return lax.dot_general(
        left, right, (((left_dim,), (right_dim,)), ((), ())), preferred_element_type=wide
    )


def unit_of(values):
    scale = lax.rsqrt(jnp.mean(values * values, axis=-1, keepdims=True) + epsilon)
    return values * scale, scale


def normalize_back(values, weighted):
    unit, scale = unit_of(values)
    grad = scale * (weighted - unit * jnp.mean(weighted * unit, axis=-1, keepdims=True))
    return grad, unit


def rotary_tables(positions):
    freqs = rotary_base ** (-2.0 * jnp.arange(HEAD // 2, dtype=wide) / HEAD)
    angles = positions.astype(wide)[:, None] * freqs[None, :]
    return jnp.cos(angles), jnp.sin(angles)


def rotate(values, cosine, sine):
    half = values.shape[-1] // 2
    front, back = values[..., :half], values[..., half:]
    return jnp.concatenate([front * cosine - back * sine, back * cosine + front * sine], axis=-1)


def gated_gelu(gate, up):
    return jax.nn.gelu(gate, approximate=True) * up


def flip(x, axis, mask):
    return lax.ppermute(x, axis, [(i, i ^ mask) for i in range(lax.axis_size(axis))])


def other_core(x):
    return flip(x, "seq", 1)


def other_x(x):
    return flip(x, "seq", 2)


def other_y(x):
    return flip(x, "tensor", 1)


def after(x, *others):
    if not others:
        return x
    nothing = sum(other[(0,) * other.ndim].astype(wide) * 0.0 for other in others)
    return x + nothing.astype(x.dtype)


PAIR = [(0, 1), (1, 0), (2, 3), (3, 2)]
MIDDLE = [(1, 2), (2, 1)]
OUTWARD = [(1, 0), (2, 3)]
INWARD = [(0, 1), (3, 2)]
ENDS = [(0, 3), (3, 0)]
END_TO_NEAR = [(0, 2), (3, 1)]
MIDDLE_TO_FAR = [(1, 3), (2, 0)]


def slot_places():
    count, place = lax.axis_size("fsdp"), lax.axis_index("fsdp")
    if count != 4:
        return [jnp.int32(i) for i in range(count)]
    first = place < 2
    return [place, place ^ 1, jnp.where(first, 2, 1), jnp.where(first, 3, 0)]


def gather_slots(piece):
    count = lax.axis_size("fsdp")
    if count != 4:
        whole = lax.all_gather(piece, "fsdp", axis=0, tiled=False)
        return [whole[i] for i in range(count)]
    pair = lax.ppermute(piece, "fsdp", PAIR)
    near = lax.ppermute(piece, "fsdp", MIDDLE)
    far = lax.ppermute(piece, "fsdp", ENDS) + lax.ppermute(piece, "fsdp", END_TO_NEAR)
    return [piece, pair, near + lax.ppermute(near, "fsdp", OUTWARD), far]


def gather_places(piece):
    count, place = lax.axis_size("fsdp"), lax.axis_index("fsdp")
    if count != 4:
        whole = lax.all_gather(piece, "fsdp", axis=0, tiled=False)
        return [(whole[i], jnp.int32(i)) for i in range(count)]
    got = [(piece, place)]
    for by in range(1, count):
        pairs = [(i, (i + by) % count) for i in range(count)]
        got.append((lax.ppermute(piece, "fsdp", pairs), (place - by) % count))
    return got


def scatter_start(pieces):
    count = lax.axis_size("fsdp")
    pieces = [p.astype(low) for p in pieces]
    if count != 4:
        return [lax.psum_scatter(jnp.stack(pieces), "fsdp", scatter_dimension=0, tiled=False)]
    own, pair, near, far = pieces
    near_in = lax.ppermute(near, "fsdp", INWARD)
    ends = lax.ppermute(far, "fsdp", ENDS)
    middle = lax.ppermute(far, "fsdp", MIDDLE_TO_FAR)
    pair_in = lax.ppermute(pair, "fsdp", PAIR)
    near = (near.astype(wide) + near_in.astype(wide)).astype(low)
    return [own, pair_in, ends, middle, lax.ppermute(near, "fsdp", MIDDLE)]


def scatter_end(got):
    total = got[0].astype(wide)
    for part in got[1:]:
        total = total + part.astype(wide)
    return total


def ordered(pieces, place):
    return [lax.select_n(place ^ i, *pieces) for i in range(len(pieces))]


def swap_masks(blocks, place):
    got = [lax.dynamic_index_in_dim(blocks, place, 0, False)]
    for mask in range(1, blocks.shape[0]):
        got.append(flip(lax.dynamic_index_in_dim(blocks, place ^ mask, 0, False), "seq", mask))
    return got


def swap_seq(blocks, place):
    return ordered(swap_masks(blocks, place), place)


def dot_nt(left, right):
    return dot(left, right, 1, 1)


def visible_of(query_doc, key_doc, query_at, key_at, same, windowed):
    seen = query_doc == key_doc
    if same:
        seen = seen & (query_at >= key_at)
    if windowed:
        seen = seen & (query_at - key_at < WINDOW)
    return seen


def tiles(blocks, line, rows, chunk):
    reach = min(blocks - 1, (WINDOW - 2 + line * rows) // (line * rows))
    return [
        [
            (key_block, slot, key_block == block)
            for key_block in range(max(0, block - reach), block + 1)
            for slot in range(0, line, chunk)
        ]
        for block in range(blocks)
    ]


def chunk_of(keyed, kind, key_block, slot, chunk):
    return jnp.concatenate([keyed[kind, slot + i, key_block] for i in range(chunk)], axis=0)


def attend_kernel(
    plan, chunk, windowed, core, query, query_doc, query_at, keyed, key_doc, key_at, out, lse
):
    line, rows = keyed.shape[1], keyed.shape[3]
    kind = core[0]
    for block, parts in enumerate(plan):
        here = pl.ds(block * rows, rows)
        q = query[here, :]
        total = jnp.zeros((rows, 1), wide)
        summed = jnp.zeros((rows, HEAD), wide)
        for key_block, slot, same in parts:
            there = pl.ds((key_block * line + slot) * rows, chunk * rows)
            scores = dot_nt(q, chunk_of(keyed, kind, key_block, slot, chunk))
            weights = jnp.exp(soft_cap * jnp.tanh(scores * (1.0 / soft_cap)))
            seen = visible_of(
                query_doc[here, :], key_doc[:, there], query_at[here, :], key_at[:, there], same, windowed
            )
            weights = jnp.where(seen, weights, 0.0)
            total = total + jnp.sum(weights, axis=1, keepdims=True)
            summed = summed + dot(
                weights.astype(low), chunk_of(keyed, 1 - kind, key_block, slot, chunk)
            )
        out[here, :] = summed / total
        lse[here, :] = jnp.log(total)


def attend_back_kernel(
    plan,
    chunk,
    windowed,
    core,
    query,
    query_doc,
    query_at,
    keyed,
    key_doc,
    key_at,
    incoming,
    lse,
    delta,
    grad_query,
    grad_keyed,
    key_total,
    value_total,
):
    line, rows = keyed.shape[1], keyed.shape[3]
    kind = core[0]
    seen_by = {}
    for block, parts in enumerate(plan):
        for key_block, slot, same in parts:
            seen_by.setdefault((key_block, slot), []).append((block, same))
    grad_query[...] = jnp.zeros_like(grad_query)
    for key_block, slot in sorted(seen_by):
        there = pl.ds((key_block * line + slot) * rows, chunk * rows)
        k = chunk_of(keyed, kind, key_block, slot, chunk)
        v = chunk_of(keyed, 1 - kind, key_block, slot, chunk)
        for turn, (block, same) in enumerate(seen_by[key_block, slot]):
            here = pl.ds(block * rows, rows)
            q = query[here, :]
            d = incoming[here, :]
            bent = jnp.tanh(dot_nt(k, q) * (1.0 / soft_cap))
            weights = jnp.exp(soft_cap * bent - lse[:, here])
            seen = visible_of(
                query_doc[:, here], key_doc[there, :], query_at[:, here], key_at[there, :], same, windowed
            )
            weights = jnp.where(seen, weights, 0.0)
            grads = weights * (dot_nt(v, d) - delta[:, here]) * (1.0 - bent * bent)
            grads = grads.astype(low)
            value_part = dot(weights.astype(low), d)
            key_part = dot(grads, q)
            if turn == 0:
                value_total[...] = value_part
                key_total[...] = key_part
            else:
                value_total[...] += value_part
                key_total[...] += key_part
            grad_query[here, :] += dot(grads, k, 0, 0)
        for i in range(chunk):
            inside = pl.ds(i * rows, rows)
            grad_keyed[kind, slot + i, key_block] = key_total[inside, :].astype(low)
            grad_keyed[1 - kind, slot + i, key_block] = value_total[inside, :].astype(low)


def in_vmem(count):
    return [pl.BlockSpec(memory_space=pltpu.SMEM)] + [pl.BlockSpec(memory_space=pltpu.VMEM)] * count


def kernel_sizes(keyed):
    _, line, blocks, rows, _ = keyed.shape
    chunk = min(line, max(1, 1024 // rows))
    plan = tiles(blocks, line, rows, chunk)
    count = sum(len(parts) for parts in plan) * rows * rows * chunk
    return plan, chunk, line * blocks * rows > WINDOW, count


def attend(core, query, docs, ats, keyed, key_docs, key_ats):
    tokens = query.shape[0]
    plan, chunk, windowed, count = kernel_sizes(keyed)
    return pl.pallas_call(
        functools.partial(attend_kernel, plan, chunk, windowed),
        out_shape=(
            jax.ShapeDtypeStruct((tokens, HEAD), wide),
            jax.ShapeDtypeStruct((tokens, 1), wide),
        ),
        in_specs=in_vmem(6),
        out_specs=(pl.BlockSpec(memory_space=pltpu.VMEM),) * 2,
        compiler_params=pltpu.CompilerParams(vmem_limit_bytes=48 * 1024 * 1024),
        cost_estimate=pl.CostEstimate(
            flops=4 * count * HEAD, bytes_accessed=2 * keyed.size, transcendentals=2 * count
        ),
        name="attend",
    )(core, query, docs, ats, keyed, key_docs, key_ats)


def attend_back(core, query, docs, ats, keyed, key_docs, key_ats, incoming, lse, delta):
    tokens = query.shape[0]
    plan, chunk, windowed, count = kernel_sizes(keyed)
    total = pltpu.VMEM((chunk * keyed.shape[3], HEAD), wide)
    return pl.pallas_call(
        functools.partial(attend_back_kernel, plan, chunk, windowed),
        out_shape=(
            jax.ShapeDtypeStruct((tokens, HEAD), wide),
            jax.ShapeDtypeStruct(keyed.shape, low),
        ),
        in_specs=in_vmem(9),
        out_specs=(pl.BlockSpec(memory_space=pltpu.VMEM),) * 2,
        scratch_shapes=[total, total],
        compiler_params=pltpu.CompilerParams(vmem_limit_bytes=56 * 1024 * 1024),
        cost_estimate=pl.CostEstimate(
            flops=10 * count * HEAD, bytes_accessed=4 * keyed.size, transcendentals=2 * count
        ),
        name="attend_back",
    )(
        core,
        query,
        docs,
        ats,
        keyed,
        key_docs,
        key_ats,
        incoming,
        lse,
        delta,
    )


def join_kernel(core, mine, theirs, out):
    ours = pl.program_id(0) == core[0]

    @pl.when(ours)
    def _():
        out[...] = mine[...].astype(wide)

    @pl.when(jnp.logical_not(ours))
    def _():
        out[...] = theirs[...].astype(wide)


def join_halves(core, mine, theirs):
    half, width = mine.shape
    rows = next(rows for rows in (288, 144, 72, half) if half % rows == 0)
    steps = half // rows
    return pl.pallas_call(
        join_kernel,
        out_shape=jax.ShapeDtypeStruct((2 * half, width), wide),
        grid_spec=pltpu.PrefetchScalarGridSpec(
            num_scalar_prefetch=1,
            grid=(2, steps),
            in_specs=[
                pl.BlockSpec((rows, width), lambda h, i, c: (jnp.where(h == c[0], i, 0), 0)),
                pl.BlockSpec((rows, width), lambda h, i, c: (jnp.where(h == c[0], 0, i), 0)),
            ],
            out_specs=pl.BlockSpec((rows, width), lambda h, i, c: (h * steps + i, 0)),
        ),
        compiler_params=pltpu.CompilerParams(vmem_limit_bytes=32 * 1024 * 1024),
        cost_estimate=pl.CostEstimate(flops=0, bytes_accessed=14 * half * width, transcendentals=0),
        name="join_halves",
    )(core, mine, theirs)


def per_device(
    layer_input,
    positions,
    gain_attn_in,
    w_query,
    w_key,
    w_value,
    w_out,
    gain_attn_out,
    gain_ffn_in,
    w_gate,
    w_up,
    w_down,
    gain_ffn_out,
    cotangent,
):
    rows, width = layer_input.shape
    half_rows = cotangent.shape[0]
    blocks = lax.axis_size("seq")
    line = lax.axis_size("fsdp")
    seq_place = lax.axis_index("seq")
    fsdp_place = lax.axis_index("fsdp")
    tensor_place = lax.axis_index("tensor")
    core = seq_place % 2
    side = seq_place // 2
    share = gain_attn_in.shape[0]
    heads = w_query.shape[1] // HEAD
    places = slot_places()
    scale = HEAD ** (-0.5)
    assert blocks == heads == 4 and w_key.shape[1] == 2 * HEAD

    query_blocks = w_query.reshape(share, blocks, HEAD).transpose(1, 0, 2)
    keyed_blocks = jnp.stack(
        [(w_key, w_value)[i % 2][:, (i // 2) * HEAD : (i // 2 + 1) * HEAD] for i in range(blocks)]
    )

    def assemble(pieces):
        whole = jnp.zeros((blocks, line, share, HEAD), low)
        for piece, at in pieces:
            whole = lax.dynamic_update_slice(whole, piece[:, None], (0, at, 0, 0))
        return whole.reshape(width, HEAD)

    from_x = other_x(layer_input)

    small = jnp.concatenate(
        [positions.astype(wide)]
        + [g.astype(wide) for g in (gain_attn_in, gain_attn_out, gain_ffn_in, gain_ffn_out)]
    )
    small = jnp.pad(small, (0, -small.shape[0] % 1024)).reshape(-1, 128)
    small_line = jnp.zeros((line,) + small.shape, wide)
    for piece, at in gather_places(small):
        small_line = lax.dynamic_update_index_in_dim(small_line, piece, at, 0)
    small_all = jnp.stack(
        ordered([small_line] + [flip(small_line, "seq", m) for m in range(1, blocks)], seq_place)
    ).reshape(blocks, line, -1)
    gain_one, gain_two, gain_three, gain_four = [
        small_all[:, :, rows + i * share : rows + (i + 1) * share].reshape(width) for i in range(4)
    ]
    place_all = small_all[:, :, :rows].astype(jnp.int32)

    keyed_piece = after(jnp.stack(swap_seq(keyed_blocks, seq_place)), from_x, gain_one)
    from_core = other_core(layer_input)
    from_far = other_core(from_x)

    keyed_w = assemble(gather_places(keyed_piece))
    query_piece = jnp.stack(swap_seq(query_blocks, seq_place))
    query_w = lax.all_gather(after(query_piece, keyed_w), "fsdp", axis=1, tiled=False).reshape(width, HEAD)

    out_w = lax.all_gather(after(w_out.T, keyed_piece), ("seq", "fsdp"), axis=0, tiled=True)

    normed = jnp.zeros((blocks, rows, width), low)
    for mask, piece in enumerate((layer_input, from_core, from_x, from_far)):
        unit = unit_of(piece.astype(wide))[0]
        normed = lax.dynamic_update_index_in_dim(
            normed, (unit * gain_one).astype(low), seq_place ^ mask, 0
        )
    normed = normed.reshape(blocks * rows, width)
    keyed_raw = dot(normed, keyed_w)

    token_rows = jnp.arange(rows, dtype=jnp.int32)
    block_starts = jnp.arange(blocks, dtype=jnp.int32)[:, None, None] * (line * rows)
    key_at = block_starts + (jnp.stack(places) * rows)[None, :, None] + token_rows
    key_places = jnp.stack(
        [lax.dynamic_index_in_dim(place_all, at, 1, False) for at in places], axis=1
    )
    key_doc = (key_at - key_places).reshape(-1)
    key_at = key_at.reshape(-1)
    own_positions = lax.dynamic_index_in_dim(place_all, fsdp_place, 1, False).reshape(-1)
    query_at = (block_starts[:, 0] + fsdp_place * rows + token_rows).reshape(-1)
    query_doc = query_at - own_positions
    cosine, sine = rotary_tables(own_positions)
    plain = core == 1

    keyed = jnp.where(plain, keyed_raw, rotate(keyed_raw, cosine, sine)).astype(low)
    keyed_slots = gather_slots(keyed.reshape(blocks, rows, HEAD))
    other_slots = [other_core(piece) for piece in keyed_slots]
    keyed_all = jnp.stack(keyed_slots + other_slots).reshape(2, line, blocks, rows, HEAD)
    query_raw = dot(normed, query_w)
    queries = (rotate(query_raw, cosine, sine) * scale).astype(low)
    core_array = core.reshape(1).astype(jnp.int32)

    attend_out, log_total = attend(
        core_array,
        queries,
        query_doc[:, None],
        query_at[:, None],
        keyed_all,
        key_doc[None, :],
        key_at[None, :],
    )
    back_marks = (query_doc[None, :], query_at[None, :], key_doc[:, None], key_at[:, None])
    log_total = log_total.reshape(1, -1)

    attended = jnp.concatenate(
        swap_seq(attend_out.astype(low).reshape(blocks, rows, HEAD), seq_place), axis=1
    )
    away = lax.dynamic_slice_in_dim(attended, (1 - tensor_place) * half_rows, half_rows, 0)
    kept = lax.dynamic_slice_in_dim(attended, tensor_place * half_rows, half_rows, 0)
    branch_away = other_y(dot(away, out_w, 1, 1).astype(low))
    branch = dot(kept, out_w, 1, 1) + branch_away.astype(wide)

    both_w = after(jnp.concatenate([query_w, keyed_w], axis=1), attended)
    both_all = lax.all_gather(both_w, "seq", axis=0, tiled=False)

    inputs_half = lax.dynamic_slice_in_dim(
        layer_input, tensor_place * half_rows, half_rows, 0
    ).astype(wide)
    middle = inputs_half + unit_of(branch)[0] * gain_two
    ffn_in = (unit_of(middle)[0] * gain_three).astype(low)

    def through(piece, work):
        if line != 4:
            parts = [
                work(jnp.concatenate([slot, other_y(slot)], axis=0)) for slot in gather_slots(piece)
            ]
            kept = [part[0] for part in parts]
            sums = [
                p[:half_rows] + other_y(p[half_rows:].astype(low)).astype(wide) for _, p in parts
            ]
            return kept, scatter_end(scatter_start(sums))

        def joined(one, two, *others):
            return after(jnp.concatenate([one, two], axis=0), *others)

        pair = lax.ppermute(piece, "fsdp", PAIR)
        near_middle = lax.ppermute(piece, "fsdp", MIDDLE)
        own_y = other_y(piece)
        pair_y = other_y(pair)
        far_middle = lax.ppermute(pair, "fsdp", MIDDLE)
        near_end = lax.ppermute(near_middle, "fsdp", OUTWARD)
        own_kept, own_part = work(joined(piece, own_y, pair, near_middle))
        near = near_middle + near_end
        near_y = other_y(near)
        far = far_middle + lax.ppermute(far_middle, "fsdp", OUTWARD)
        pair_kept, pair_part = work(joined(pair, pair_y, near, far_middle))
        far_y = other_y(far)
        near_kept, near_part = work(joined(near, near_y, far))
        far_kept, far_part = work(joined(far, far_y, near_part))
        kept = (own_kept, pair_kept, near_kept, far_kept)

        def sent(part, *others):
            return other_y(after(part[half_rows:].astype(low), *others))

        def added(part, got, *others):
            return after(part[:half_rows] + got.astype(wide), *others).astype(low)

        near_got = sent(near_part)
        far_got = sent(far_part)
        pair_got = sent(pair_part, far_part, near_got)
        own_got = sent(own_part, far_got)
        near_sum = added(near_part, near_got)
        near_in = lax.ppermute(near_sum, "fsdp", INWARD)
        far_sum = added(far_part, far_got)
        far_ends = lax.ppermute(far_sum, "fsdp", ENDS)
        far_middle = lax.ppermute(far_sum, "fsdp", MIDDLE_TO_FAR)
        near_sum = (near_sum.astype(wide) + near_in.astype(wide)).astype(low)
        near_middle = lax.ppermute(near_sum, "fsdp", MIDDLE)
        pair_sum = added(pair_part, pair_got)
        pair_in = lax.ppermute(pair_sum, "fsdp", PAIR)
        total = own_part[:half_rows]
        for part in (own_got, near_middle, far_ends, far_middle, pair_in):
            total = total + part.astype(wide)
        return kept, total

    def forward(part):
        gate, up = dot(part, w_gate), dot(part, w_up)
        hidden = gated_gelu(gate, up).astype(low)
        return (part, gate, up, hidden), dot(hidden, w_down)

    forward_kept, ffn_out = through(ffn_in, forward)
    ffn_out = after(ffn_out, both_all)
    unit_out, _ = unit_of(ffn_out)
    output = middle + unit_out * gain_four

    incoming = cotangent.astype(wide)
    grad_ffn_out, _ = normalize_back(ffn_out, incoming * gain_four)
    gain_four_part = jnp.sum(incoming * unit_out, axis=0)
    still = list(forward_kept)

    def backward(part):
        _, gate, up, _ = still.pop(0)
        _, pullback = jax.vjp(gated_gelu, gate, up)
        grad_gate, grad_up = pullback(dot(part, w_down, 1, 1))
        grad_gate, grad_up = grad_gate.astype(low), grad_up.astype(low)
        return (part, grad_gate, grad_up), dot(grad_gate, w_gate, 1, 1) + dot(grad_up, w_up, 1, 1)

    rows_all = jnp.concatenate([k[0] for k in forward_kept], axis=0)
    hidden_all = jnp.concatenate([k[3] for k in forward_kept], axis=0)

    def rows_product(left, rights, *others):
        return dot(left, after(jnp.concatenate(rights, axis=0), *others), 0, 0).astype(low)

    def core_half(grad):
        half = grad.shape[0] // 2
        sent = lax.dynamic_slice_in_dim(grad, (1 - core) * half, half, 0)
        kept = lax.dynamic_slice_in_dim(grad, core * half, half, 0)
        return (kept.astype(wide) + other_core(sent).astype(wide)).astype(low)

    def over_x(mine, sides=((0, 2), (1, 3))):
        return lax.psum(mine, "seq", axis_index_groups=[list(side) for side in sides])


    backward_kept, grad_ffn_in = through(grad_ffn_out.astype(low), backward)

    grad_mid_norm, unit_middle = normalize_back(middle, grad_ffn_in * gain_three)
    gain_three_part = jnp.sum(grad_ffn_in * unit_middle, axis=0)
    grad_middle = incoming + grad_mid_norm
    grad_branch, unit_branch = normalize_back(branch, grad_middle * gain_two)
    gain_two_part = jnp.sum(grad_middle * unit_branch, axis=0)
    grad_branch = grad_branch.astype(low)
    gain_parts = jnp.stack([gain_two_part, gain_three_part, gain_four_part])
    branch_other = other_y(grad_branch)

    down_mine = core_half(rows_product(hidden_all, [k[0] for k in backward_kept], branch_other))
    gate_mine = core_half(rows_product(rows_all, [k[1] for k in backward_kept], grad_branch))
    up_mine = core_half(rows_product(rows_all, [k[2] for k in backward_kept], branch_other))
    down_sum, gate_sum = over_x((down_mine, gate_mine))

    always = positions[0] >= 0

    def stretch(work):
        shapes = jax.eval_shape(work)
        return lax.cond(
            always, work, lambda: jax.tree.map(lambda x: jnp.zeros(x.shape, x.dtype), shapes)
        )

    def attention_back():
        gains = gain_parts + other_y(gain_parts)
        first = tensor_place == 0
        branch_cot = jnp.concatenate(
            [
                jnp.where(first, grad_branch, branch_other),
                jnp.where(first, branch_other, grad_branch),
            ],
            axis=0,
        )
        grad_attended = dot(branch_cot, out_w).astype(low)
        grad_attended = jnp.concatenate(
            swap_seq(grad_attended.reshape(rows, blocks, HEAD).transpose(1, 0, 2), seq_place), axis=0
        )
        delta = jnp.sum(attend_out * grad_attended.astype(wide), axis=1)
        grad_queries, grad_keyed = attend_back(
            core_array,
            queries,
            *back_marks[:2],
            keyed_all,
            *back_marks[2:],
            grad_attended,
            log_total,
            delta[None, :],
        )
        keyed_got = other_core(grad_keyed[1])
        keyed_started = scatter_start(
            [grad_keyed[0, i].astype(wide) + keyed_got[i].astype(wide) for i in range(line)]
        )
        grad_query_raw = rotate(grad_queries * scale, cosine, -sine).astype(low)

        extra = 16
        gain_rows = gains.reshape(3, 2, 2, line, share).transpose(2, 3, 1, 0, 4)
        gain_rows = gain_rows.reshape(2, line, 2, 1, 3 * share).astype(low)
        gain_rows = jnp.pad(
            gain_rows, ((0, 0),) * 3 + ((0, extra - 1), (0, heads * HEAD - 3 * share))
        )
        out_grad = dot(after(branch_cot, grad_queries), attended, 0, 0).astype(low)
        out_grad = out_grad.reshape(2, 2, line, share, heads * HEAD).transpose(1, 2, 0, 3, 4)
        out_grad = jnp.concatenate([out_grad, gain_rows], axis=3)
        out_got = other_core(lax.dynamic_index_in_dim(out_grad, 1 - core, 0, False))
        out_sum = lax.dynamic_index_in_dim(out_grad, core, 0, False).astype(wide)
        out_sum = (out_sum + out_got.astype(wide)).astype(low)

        keyed_own = scatter_end(keyed_started).reshape(blocks * rows, HEAD)
        grad_keyed_raw = jnp.where(plain, keyed_own, rotate(keyed_own, cosine, -sine)).astype(low)
        return jnp.concatenate([grad_query_raw, grad_keyed_raw], axis=1), out_sum

    grad_raw, out_sum = stretch(attention_back)

    weight_grad = dot(normed, grad_raw, 0, 0).astype(low).reshape(blocks, line, share, 2 * HEAD)
    weight_started = scatter_start(
        [lax.dynamic_index_in_dim(weight_grad, at, 1, False) for at in places]
    )

    up_sum = over_x(after(up_mine, weight_started[:2][-1]), ((1, 3), (0, 2)))
    grad_gate_w, grad_down_w = [
        join_halves(core_array, mine, other_core(mine)) for mine in (gate_sum, down_sum)
    ]

    raw_mine = swap_seq(grad_raw.reshape(blocks, rows, 2 * HEAD), seq_place)
    back = sum(dot(part, both_all[i], 1, 1) for i, part in enumerate(raw_mine))
    back_got = other_y(
        lax.dynamic_slice_in_dim(back, (1 - tensor_place) * half_rows, half_rows, 0).astype(low)
    )
    back = lax.dynamic_slice_in_dim(back, tensor_place * half_rows, half_rows, 0)
    back = after(back, grad_gate_w, grad_down_w) + back_got.astype(wide)
    grad_input = grad_middle + normalize_back(inputs_half, back * gain_one)[0]

    out_parts = after(out_sum, weight_grad)
    out_started = scatter_start(
        [lax.dynamic_index_in_dim(out_parts, at, 0, False) for at in places]
    )
    weight_sum = scatter_end(weight_started).astype(low)
    out_sum = scatter_end(out_started)
    out_got = other_x(lax.dynamic_index_in_dim(out_sum, 1 - side, 0, False).astype(low))
    weight_grads = [part.astype(wide) for part in swap_seq(weight_sum, seq_place)]
    query_grads = jnp.concatenate([part[:, :HEAD] for part in weight_grads], axis=1)
    key_grads = jnp.concatenate([part[:, HEAD:] for part in weight_grads[0::2]], axis=1)
    value_grads = jnp.concatenate([part[:, HEAD:] for part in weight_grads[1::2]], axis=1)
    gain_one_part = (
        jnp.sum(query_grads * w_query.astype(wide), axis=1)
        + jnp.sum(key_grads * w_key.astype(wide), axis=1)
        + jnp.sum(value_grads * w_value.astype(wide), axis=1)
    )
    grad_gain_one = (gain_one_part + other_y(gain_one_part)) / gain_attn_in.astype(wide)
    out_sum = lax.dynamic_index_in_dim(out_sum, side, 0, False) + out_got.astype(wide)
    gain_sums = out_sum[share, : 3 * share].reshape(3, share)

    return (
        output.astype(low),
        grad_input,
        grad_gain_one,
        query_grads,
        key_grads,
        value_grads,
        out_sum[:share].T,
        gain_sums[0],
        gain_sums[1],
        grad_gate_w,
        join_halves(core_array, up_sum, other_core(up_sum)),
        grad_down_w,
        gain_sums[2],
    )


def solution(mesh):
    by_rows = P(("seq", "fsdp"))
    placed = (
        P(("seq", "fsdp"), None),
        by_rows,
        by_rows,
        P(("seq", "fsdp"), "tensor"),
        P(("seq", "fsdp"), "tensor"),
        P(("seq", "fsdp"), "tensor"),
        P("tensor", ("seq", "fsdp")),
        by_rows,
        by_rows,
        P(None, ("fsdp", "tensor")),
        P(None, ("fsdp", "tensor")),
        P(("fsdp", "tensor"), None),
        by_rows,
        P(("seq", "fsdp", "tensor"), None),
    )
    return jax.shard_map(
        per_device,
        mesh=mesh,
        in_specs=placed,
        out_specs=(
            P(("seq", "fsdp", "tensor"), None),
            P(("seq", "fsdp", "tensor"), None),
            by_rows,
            P(("seq", "fsdp"), "tensor"),
            P(("seq", "fsdp"), "tensor"),
            P(("seq", "fsdp"), "tensor"),
            P("tensor", ("seq", "fsdp")),
            by_rows,
            by_rows,
            P(None, ("fsdp", "tensor")),
            P(None, ("fsdp", "tensor")),
            P(("fsdp", "tensor"), None),
            by_rows,
        ),
        check_vma=False,
    )
```
